32 devices in a mesh: tiles: 16 (over z, y, x), lev: 2 (over core).
Axes of the slice: x: 2, y: 2, z: 4, core: 2. Of those that a mesh axis runs over, the one named last changes fastest.
Arguments:
- atm_anom: bfloat16 [16, 30, 65536], P('lev', None, 'tiles'), may hold values from -6 to 6
- ocn_anom: bfloat16 [20, 30, 393216], P('lev', None, 'tiles'), may hold values from -6 to 6
- remap_w: bfloat16 [1024, 128, 128], P('tiles'), may hold values from -0.5 to 0.5
- rem_tile: int32 [1024, 1], P('tiles'), may hold values from 0 to 15; in each aligned block of 64 rows (0 to 63, 64 to 127, ...) at most 8 rows name the same one
- rem_block: int32 [1024], P('tiles'), may hold values from 0 to 191
- obs_weight: bfloat16 [16, 393216], P('lev', 'tiles'), may hold values from -1.5 to 1.5
- innov_ocn: float32 [393216], P('tiles'), may hold values from -6 to 6
- innov_atm: float32 [65536], P('tiles'), may hold values from -6 to 6
- band_ocn: int32 [393216], P('tiles'), may hold values from 0 to 19
- band_atm: int32 [65536], P('tiles'), may hold values from 0 to 15
Outputs:
- ocn_increment: float32 [20, 393216], P('lev', 'tiles')
- atm_increment: float32 [16, 65536], P('lev', 'tiles')
The draws below stay inside these ranges and needn't reach their ends.
Inputs may be any that keep to these rules, and one draw needn't show every extreme that they name: `rem_tile`: in each tile's 64 remap blocks no ocean tile is named more than 8 times, a bound that some block reaches.
All inputs are finite; a program needn't handle non-finite values.
Results may differ from the reference program's by a relative error of at most 0.003.
Values may be sent and summed in bfloat16 or wider, within the bound.
A program may use at most 128 MiB of HBM per device.

```python
import math
import jax
import jax.numpy as jnp
import numpy as np
from jax import lax

MEM = 30
ALEV = 16
OLEV = 20
BLK = 128
ABLK = 32
OBLK = 192
RPB = 2
LTAP = 8
NREM = 64
CAP = 8
NREM_TOT = 1024
ACELLS = 65536
OCELLS = 393216
N_TILES = 16


def plant(array, rng, least, top_value):
    spot = [jax.random.randint(jax.random.fold_in(rng, axis), (), 0, length) for axis, length in enumerate(array.shape)]
    widest = array.shape.index(max(array.shape))
    neighbour = spot[:widest] + [(spot[widest] + 1) % array.shape[widest]] + spot[widest + 1:]
    return array.at[tuple(spot)].set(least).at[tuple(neighbour)].set(top_value)


def level_of(own_key, extent, pieces, smallest, high):
    def one(dim, blocks):
        draws = jax.random.uniform(jax.random.fold_in(jax.random.fold_in(own_key, 6), dim), (blocks,), jnp.float32, smallest / len(pieces), high / len(pieces))
        return jnp.repeat(jnp.exp(draws), extent[dim] // blocks).reshape((-1,) + (1,) * (len(extent) - dim - 1))

    loudness = one(*pieces[0])
    for cut in pieces[1:]:
        loudness = loudness * one(*cut)
    return loudness


def deal_out(own_key, own, number, rows, count, top, limit, lean):
    sequence = jax.random.permutation(own_key, count)
    heavy_load, usual = shares(count, rows * top, limit, lean, True), shares(count, rows * top, limit, lean, False)
    places = jnp.arange(count)

    def named(tallies, turn):
        used = int((tallies > 0).sum())
        fixed = max(1, used // 4)
        passed = fixed + (places - fixed + turn * (used - fixed)) % max(1, count - fixed)
        return jnp.zeros((count,), jnp.int32).at[sequence[jnp.where(places < fixed, places, passed)]].set(jnp.asarray(tallies, jnp.int32))

    tallies = jnp.where(number % 4 == 0, named(heavy_load, number // 4), named(usual, number - number // 4 - 1))
    mixed = jax.random.permutation(jax.random.fold_in(own, 3), count)
    donor, taker = mixed[0:count // 2 * 2:2], mixed[1:count // 2 * 2:2]
    room = jnp.minimum(tallies[donor] - 1, limit - tallies[taker]) // 2
    room = jnp.where((donor == sequence[0]) | (taker == sequence[0]) | (tallies[taker] == 0), 0, jnp.maximum(room, 0))
    passed = jax.random.randint(jax.random.fold_in(own, 4), (count // 2,), 0, 1 << 20) % (room + 1)
    tallies = tallies.at[donor].add(-passed).at[taker].add(passed)
    items = jnp.searchsorted(jnp.cumsum(tallies), jnp.arange(rows * top), side="right").astype(jnp.int32)
    grid = items.reshape(top, rows).T
    grid = grid[jax.random.permutation(jax.random.fold_in(own, 1), rows)]
    turn = jax.random.randint(jax.random.fold_in(own, 2), (rows, 1), 0, top)
    return jnp.take_along_axis(grid, (jnp.arange(top)[None, :] + turn) % top, axis=1)


def shares(count, total, most, lean, full):
    portions = [(1 << 20) // math.isqrt(rank ** lean) + 1 for rank in range(1, count + 1)]
    largest = most if full else min(most, max(-(-total // count), total * portions[0] // sum(portions)))
    least = 1 if total - largest >= count - 1 else 0
    given, rest = [largest] + [least] * (count - 1), total - largest - least * (count - 1)
    while rest > 0:
        candidates = [i for i in range(1, count) if given[i] < largest] or [i for i in range(1, count) if given[i] < most]
        pool, remaining = sum([portions[i] for i in candidates]), rest
        for i in candidates:
            more = min(most - given[i], max(1, remaining * portions[i] // pool), rest)
            given[i] = given[i] + more
            rest = rest - more
    return np.array(given)


def bell_draw(rng, shape, width, reach, pieces=(), held_as=jnp.bfloat16):
    gain = level_of(rng, shape, pieces, -0.22, 0.18) if pieces else 1.0
    result = jax.random.normal(rng, shape, jnp.float32) * width * gain
    return jnp.minimum(jnp.maximum(result, -reach), reach).astype(held_as)


def setup_inputs(seed: int = 0) -> dict:
    keys = jax.random.split(jax.random.key(seed), 11)
    atm_anom = bell_draw(keys[0], (ALEV, MEM, ACELLS), 1.0, 6.0, ((0, 2), (2, 16)))
    ocn_anom = bell_draw(keys[1], (OLEV, MEM, OCELLS), 1.0, 6.0, ((0, 2), (2, 16)))
    remap_w = bell_draw(keys[2], (NREM_TOT, BLK, BLK), BLK ** -0.5, 0.5, ((0, 16),))
    rem_tile_keys = jax.random.split(jax.random.fold_in(keys[3], 1), NREM_TOT // NREM)
    rem_tile_turns = jax.random.permutation(jax.random.fold_in(keys[3], 3), NREM_TOT // NREM)
    rem_tile = jax.vmap(lambda own, number: deal_out(jax.random.fold_in(keys[3], 2), own, number, NREM, N_TILES, 1, CAP, 2))(rem_tile_keys, rem_tile_turns).reshape((NREM_TOT, 1))
    rem_block = plant(jax.random.randint(keys[4], (NREM_TOT,), 0, OBLK), jax.random.fold_in(keys[4], 1), 0, OBLK - 1).astype(jnp.int32)
    obs_weight = bell_draw(keys[5], (ALEV, OCELLS), 0.25, 1.5, ((0, 2), (1, 16)))
    innov_ocn = bell_draw(keys[6], (OCELLS,), 1.0, 6.0, ((0, 16),), jnp.float32)
    innov_atm = bell_draw(keys[7], (ACELLS,), 1.0, 6.0, ((0, 16),), jnp.float32)
    band_ocn = plant(jax.random.randint(keys[8], (OCELLS,), 0, OLEV), jax.random.fold_in(keys[8], 1), 0, OLEV - 1).astype(jnp.int32)
    band_atm = plant(jax.random.randint(keys[9], (ACELLS,), 0, ALEV), jax.random.fold_in(keys[9], 1), 0, ALEV - 1).astype(jnp.int32)
    return {"atm_anom": atm_anom, "ocn_anom": ocn_anom, "remap_w": remap_w, "rem_tile": rem_tile, "rem_block": rem_block, "obs_weight": obs_weight, "innov_ocn": innov_ocn, "innov_atm": innov_atm, "band_ocn": band_ocn, "band_atm": band_atm}


def taper(levels, band):
    lvl = jnp.arange(levels, dtype=jnp.float32)[:, None]
    return jnp.maximum(0.0, 1.0 - jnp.abs(lvl - band[None, :].astype(jnp.float32)) / LTAP)


def increment(anom, proj, band, innov, levels):
    cov = jnp.sum(anom.astype(jnp.float32) * proj[None], axis=1) / (MEM - 1)
    var = jnp.sum(proj * proj, axis=0) / (MEM - 1) + 0.1
    return taper(levels, band) * cov * (innov / var)[None, :]


def reference(atm_anom, ocn_anom, remap_w, rem_tile, rem_block, obs_weight, innov_ocn, innov_atm, band_ocn, band_atm):
    ntiles = N_TILES
    nrem = ABLK * RPB
    layer_mean = jnp.sum(ocn_anom.astype(jnp.float32), axis=0) / OLEV
    layer_blocks = layer_mean.astype(jnp.bfloat16).reshape(MEM, ntiles * OBLK, 128).transpose(1, 0, 2)
    weight_blocks = obs_weight.astype(jnp.float32).reshape(ALEV, ntiles * OBLK, 128)

    def per_tile(carry, tile):
        start = (tile * ABLK * 128).astype(jnp.int32)
        xa = lax.dynamic_slice_in_dim(atm_anom, start, ABLK * 128, 2)
        blocks = xa.reshape(ALEV, MEM, ABLK, 128).transpose(2, 0, 1, 3)
        source = jnp.repeat(blocks, RPB, axis=0).astype(jnp.float32)
        first = (tile * nrem).astype(jnp.int32)
        weights = lax.dynamic_slice_in_dim(remap_w, first, nrem, 0).astype(jnp.float32)
        dest = lax.dynamic_slice_in_dim(rem_tile[:, 0], first, nrem, 0)
        target = lax.dynamic_slice_in_dim(rem_block, first, nrem, 0)
        owner = (dest * OBLK + target).astype(jnp.int32)
        remapped = jnp.einsum('ilmc,icd->ilmd', source, weights).astype(jnp.bfloat16)
        remapped = lax.optimization_barrier(remapped).astype(jnp.float32)
        local_weight = weight_blocks[:, owner, :]
        contrib = jnp.einsum('ilmd,lid->imd', remapped, local_weight)
        carry = carry.at[owner].add(contrib)
        back = layer_blocks[owner].astype(jnp.float32)
        atm_part = jnp.einsum('imd,icd->imc', back, weights).reshape(ABLK, RPB, MEM, 128).sum(axis=1)
        return carry, atm_part

    proj_blocks, atm_parts = lax.scan(per_tile, jnp.zeros((ntiles * OBLK, MEM, 128), jnp.float32), jnp.arange(ntiles, dtype=jnp.int32))
    proj = proj_blocks.transpose(1, 0, 2).reshape(MEM, ntiles * OBLK * 128)
    ocn_on_atm = atm_parts.transpose(2, 0, 1, 3).reshape(MEM, ntiles * ABLK * 128)
    ocn_increment = increment(ocn_anom, proj, band_ocn, innov_ocn, OLEV)
    atm_increment = increment(atm_anom, ocn_on_atm, band_atm, innov_atm, ALEV)
    return ocn_increment, atm_increment
```

```python
import functools

import jax
import jax.numpy as jnp
from jax import lax
from jax.experimental import pallas as pl
from jax.experimental.pallas import tpu as pltpu
from jax.sharding import PartitionSpec as P

MEM = 30
HALF = 16
OLEV = 20
LTAP = 8
MESH = pl.DeviceIdType.MESH
VLIM = 56 * 1024 * 1024


def layer_kernel(x_ref, out_ref):
    total = x_ref[0].astype(jnp.float32)
    for level in range(1, x_ref.shape[0]):
        total = total + x_ref[level].astype(jnp.float32)
    out_ref[0] = total[:HALF]
    out_ref[1, : MEM - HALF, :] = total[HALF:]
    out_ref[1, MEM - HALF :, :] = jnp.zeros((2 * HALF - MEM, total.shape[1]), jnp.float32)


def layer_parts(ocn_anom, chunk):
    lev, mem, cells = ocn_anom.shape
    return pl.pallas_call(
        layer_kernel,
        grid=(cells // chunk,),
        in_specs=[pl.BlockSpec((lev, mem, chunk), lambda i: (0, 0, i))],
        out_specs=pl.BlockSpec((2, HALF, chunk), lambda i: (0, 0, i)),
        out_shape=jax.ShapeDtypeStruct((2, HALF, cells), jnp.float32),
        compiler_params=pltpu.CompilerParams(vmem_limit_bytes=VLIM),
        cost_estimate=pl.CostEstimate(
            flops=lev * mem * cells, bytes_accessed=2 * lev * mem * cells, transcendentals=0
        ),
    )(ocn_anom)


def greet(nt, me, lev):
    barrier = pltpu.get_barrier_semaphore()

    def signal(k, carry):
        pl.semaphore_signal(
            barrier, inc=1, device_id=(lax.rem(me + k, nt), lev), device_id_type=MESH
        )
        return carry

    lax.fori_loop(1, nt, signal, 0)
    pl.semaphore_signal(barrier, inc=1, device_id=(me, 1 - lev), device_id_type=MESH)
    pl.semaphore_wait(barrier, nt)


def answer_kernel(
    nt, per, part_ref, idx_ref, obs_ref,
    lay_ref, w_ref, blk_ref,
    peer, layer, obs, lay_out, w_out, blk_smem,
    peer_sems, smem_sem, idx_send, idx_recv, w_send, w_recv, lay_send, lay_recv,
):
    me, lev = lax.axis_index("tiles"), lax.axis_index("lev")
    oblk = layer.shape[0]
    greet(nt, me, lev)
    swap = pltpu.make_async_remote_copy(
        src_ref=part_ref.at[1 - lev], dst_ref=peer, send_sem=peer_sems.at[0],
        recv_sem=peer_sems.at[1], device_id=(me, 1 - lev), device_id_type=MESH,
    )
    swap.start()

    def move(src, dst, send, recv, k):
        to = lax.rem(me + k, nt)
        return pltpu.make_async_remote_copy(
            src_ref=src.at[to], dst_ref=dst.at[me], send_sem=send.at[k], recv_sem=recv.at[k],
            device_id=(to, lev), device_id_type=MESH,
        )

    def arrival(src, dst, send, recv, k):
        frm = lax.rem(me + nt - k, nt)
        return pltpu.make_async_remote_copy(
            src_ref=src.at[frm], dst_ref=dst.at[frm], send_sem=send.at[k], recv_sem=recv.at[k],
            device_id=(frm, lev), device_id_type=MESH,
        )

    idx_set = (idx_ref, blk_ref, idx_send, idx_recv)
    w_set = (w_out, w_ref, w_send, w_recv)
    lay_set = (lay_out, lay_ref, lay_send, lay_recv)

    def each(fn):
        def body(k, carry):
            fn(k)
            return carry

        lax.fori_loop(1, nt, body, 0)

    each(lambda k: move(*idx_set, k).start())

    def lanes(o):
        return pl.ds(pl.multiple_of(o * 128, 128), 128)

    def widen(o, carry):
        obs[o] = obs_ref[:, lanes(o)].astype(jnp.float32)
        return carry

    lax.fori_loop(0, oblk, widen, 0)
    blk_ref[me] = idx_ref[me]
    each(lambda k: arrival(*idx_set, k).wait_recv())
    each(lambda k: move(*idx_set, k).wait_send())
    down = pltpu.make_async_copy(blk_ref, blk_smem, smem_sem)
    down.start()
    down.wait()

    def fill_w(to, dst):
        for s in range(0, per, 2):
            pair = [obs[blk_smem[to, s + j, 0]] for j in range(2)]
            dst[to, 8 * s : 8 * s + 16, :] = jnp.concatenate(pair, axis=0).astype(jnp.bfloat16)

    def fill_lay(to, dst):
        for s in range(per):
            dst[to, HALF * s : HALF * (s + 1), :] = layer[blk_smem[to, s, 0]]

    def send_w(k):
        fill_w(lax.rem(me + k, nt), w_out)
        move(*w_set, k).start()

    each(send_w)
    fill_w(me, w_ref)
    swap.wait()

    def mean(o, carry):
        at = lanes(o)
        layer[o] = ((part_ref[lev, :, at] + peer[:, at]) / OLEV).astype(jnp.bfloat16)
        return carry

    lax.fori_loop(0, oblk, mean, 0)

    def send_lay(k):
        fill_lay(lax.rem(me + k, nt), lay_out)
        move(*lay_set, k).start()

    each(send_lay)
    fill_lay(me, lay_ref)
    each(lambda k: arrival(*w_set, k).wait_recv())
    each(lambda k: arrival(*lay_set, k).wait_recv())
    each(lambda k: move(*w_set, k).wait_send())
    each(lambda k: move(*lay_set, k).wait_send())


def answers(part, idx, obs, nt, per):
    cells = part.shape[2]
    vmem = pl.BlockSpec(memory_space=pltpu.VMEM)
    dma = pltpu.SemaphoreType.DMA
    return pl.pallas_call(
        functools.partial(answer_kernel, nt, per),
        out_shape=(
            jax.ShapeDtypeStruct((nt, per * HALF, 128), jnp.bfloat16),
            jax.ShapeDtypeStruct((nt, per * 8, 128), jnp.bfloat16),
            jax.ShapeDtypeStruct((nt, 8, 128), jnp.int32),
        ),
        in_specs=[vmem] * 3,
        out_specs=(vmem,) * 3,
        scratch_shapes=[
            pltpu.VMEM((HALF, cells), jnp.float32),
            pltpu.VMEM((cells // 128, HALF, 128), jnp.bfloat16),
            pltpu.VMEM((cells // 128, 8, 128), jnp.float32),
            pltpu.VMEM((nt, per * HALF, 128), jnp.bfloat16),
            pltpu.VMEM((nt, per * 8, 128), jnp.bfloat16),
            pltpu.SMEM((nt, 8, 128), jnp.int32),
            dma((2,)),
            dma,
        ]
        + [dma((nt,))] * 6,
        compiler_params=pltpu.CompilerParams(
            collective_id=0, has_side_effects=True, vmem_limit_bytes=VLIM
        ),
    )(part, idx, obs)


def remap_kernel(group, rpb, slot_ref, x_ref, w_ref, lay_ref, obs_ref, con_ref, oa_ref, xs):
    lev = x_ref.shape[0]
    i = pl.program_id(0)

    @pl.when(i == 0)
    def _():
        xs[...] = jnp.zeros_like(xs)

    xs[:, :MEM, :] = x_ref[...]
    for j in range(group):
        weights = jnp.concatenate([w_ref[j * rpb + r] for r in range(rpb)], axis=1)
        x = xs[:, :, 128 * j : 128 * (j + 1)].reshape(lev * 2 * HALF, 128)
        y = jnp.dot(x, weights, preferred_element_type=jnp.float32)
        y = y.astype(jnp.bfloat16).astype(jnp.float32).reshape(lev, 2 * HALF, rpb * 128)
        obs, lay = [], []
        for r in range(rpb):
            slot = slot_ref[(i * group + j) * rpb + r]
            pair = obs_ref[pl.ds(pl.multiple_of((slot // 2) * 16, 16), 16), :].astype(jnp.float32)
            obs.append(jnp.where(slot % 2 == 0, pair[:8], pair[8:]))
            lay.append(lay_ref[pl.ds(pl.multiple_of(slot * HALF, HALF), HALF), :])
        obs = jnp.concatenate(obs, axis=1)
        total = y[0] * obs[0:1]
        for level in range(1, lev):
            total = total + y[level] * obs[level : level + 1]
        for r in range(rpb):
            for h in range(2):
                con_ref[h, j * rpb + r] = total[h * HALF : (h + 1) * HALF, 128 * r : 128 * (r + 1)]
        oa_ref[:, 128 * j : 128 * (j + 1)] = lax.dot_general(
            jnp.concatenate(lay, axis=1), weights, (((1,), (1,)), ((), ())),
            preferred_element_type=jnp.float32,
        )


def remap(slot_of, atm_anom, remap_w, lay, obs, group):
    lev, mem, cells = atm_anom.shape
    ablk, nrem = cells // 128, remap_w.shape[0]
    rpb = nrem // ablk
    lay, obs = lay.reshape(-1, 128), obs.reshape(-1, 128)
    return pl.pallas_call(
        functools.partial(remap_kernel, group, rpb),
        grid_spec=pltpu.PrefetchScalarGridSpec(
            num_scalar_prefetch=1,
            grid=(ablk // group,),
            in_specs=[
                pl.BlockSpec((lev, mem, 128 * group), lambda i, s: (0, 0, i)),
                pl.BlockSpec((rpb * group, 128, 128), lambda i, s: (i, 0, 0)),
                pl.BlockSpec(lay.shape, lambda i, s: (0, 0)),
                pl.BlockSpec(obs.shape, lambda i, s: (0, 0)),
            ],
            out_specs=[
                pl.BlockSpec((2, rpb * group, HALF, 128), lambda i, s: (0, i, 0, 0)),
                pl.BlockSpec((HALF, 128 * group), lambda i, s: (0, i)),
            ],
            scratch_shapes=[pltpu.VMEM((lev, 2 * HALF, 128 * group), jnp.bfloat16)],
        ),
        out_shape=[
            jax.ShapeDtypeStruct((2, nrem, HALF, 128), jnp.float32),
            jax.ShapeDtypeStruct((HALF, cells), jnp.float32),
        ],
        compiler_params=pltpu.CompilerParams(vmem_limit_bytes=VLIM),
        cost_estimate=pl.CostEstimate(
            flops=2 * nrem * lev * 32 * 128 * 128, bytes_accessed=8 << 20, transcendentals=0
        ),
    )(slot_of, atm_anom, remap_w, lay, obs)


def return_kernel(
    nt, per, src_ref, con_ref, oa_ref,
    got_ref, oa_out,
    peer, summed, out, peer_sems, oa_sems, send, recv, fsend, frecv,
):
    me, lev = lax.axis_index("tiles"), lax.axis_index("lev")
    greet(nt, me, lev)
    partner = (me, 1 - lev)
    swap = pltpu.make_async_remote_copy(
        src_ref=con_ref.at[1 - lev], dst_ref=peer, send_sem=peer_sems.at[0],
        recv_sem=peer_sems.at[1], device_id=partner, device_id_type=MESH,
    )
    swap.start()
    oa_swap = pltpu.make_async_remote_copy(
        src_ref=oa_ref, dst_ref=oa_out.at[lev], send_sem=oa_sems.at[0],
        recv_sem=oa_sems.at[1], device_id=partner, device_id_type=MESH,
    )
    oa_swap.start()
    oa_out[lev] = oa_ref[...]
    swap.wait()

    def add(i, carry):
        at = pl.ds(i * 8, 8)
        summed[at] = (con_ref[lev, at] + peer[at]).astype(jnp.bfloat16)
        return carry

    lax.fori_loop(0, con_ref.shape[1] // 8, add, 0)

    def move(k):
        to = lax.rem(me + k, nt)
        return pltpu.make_async_remote_copy(
            src_ref=out.at[to], dst_ref=got_ref.at[lev, me], send_sem=send.at[k],
            recv_sem=recv.at[k], device_id=(to, lev), device_id_type=MESH,
        )

    def arrival(k):
        frm = lax.rem(me + nt - k, nt)
        return pltpu.make_async_remote_copy(
            src_ref=out.at[frm], dst_ref=got_ref.at[lev, frm], send_sem=send.at[k],
            recv_sem=recv.at[k], device_id=(frm, lev), device_id_type=MESH,
        )

    def forward(k, half):
        frm = lax.rem(me + nt - k, nt)
        return pltpu.make_async_remote_copy(
            src_ref=got_ref.at[half, frm], dst_ref=got_ref.at[half, frm], send_sem=fsend.at[k],
            recv_sem=frecv.at[k], device_id=partner, device_id_type=MESH,
        )

    def start(k, carry):
        to = lax.rem(me + k, nt)
        for s in range(per):
            out[to, s * HALF : (s + 1) * HALF, :] = summed[src_ref[to * per + s]]
        move(k).start()
        return carry

    lax.fori_loop(1, nt, start, 0)
    for s in range(per):
        got_ref[lev, me, s * HALF : (s + 1) * HALF, :] = summed[src_ref[me * per + s]]
    forward(0, lev).start()

    def pass_on(k, carry):
        arrival(k).wait_recv()
        forward(k, lev).start()
        return carry

    lax.fori_loop(1, nt, pass_on, 0)

    def finish(k, carry):
        forward(k, 1 - lev).wait_recv()
        forward(k, lev).wait_send()
        return carry

    lax.fori_loop(0, nt, finish, 0)

    def sent(k, carry):
        move(k).wait_send()
        return carry

    lax.fori_loop(1, nt, sent, 0)
    oa_swap.wait()


def give_back(slot_src, con, oa, nt, per):
    nrem = con.shape[1]
    vmem = pl.BlockSpec(memory_space=pltpu.VMEM)
    dma = pltpu.SemaphoreType.DMA
    return pl.pallas_call(
        functools.partial(return_kernel, nt, per),
        out_shape=(
            jax.ShapeDtypeStruct((2, nt, per * HALF, 128), jnp.bfloat16),
            jax.ShapeDtypeStruct((2,) + oa.shape, jnp.float32),
        ),
        in_specs=[pl.BlockSpec(memory_space=pltpu.SMEM), vmem, vmem],
        out_specs=(vmem, vmem),
        scratch_shapes=[
            pltpu.VMEM((nrem, HALF, 128), jnp.float32),
            pltpu.VMEM((nrem, HALF, 128), jnp.bfloat16),
            pltpu.VMEM((nt, per * HALF, 128), jnp.bfloat16),
            dma((2,)),
            dma((2,)),
        ]
        + [dma((nt,))] * 4,
        compiler_params=pltpu.CompilerParams(
            collective_id=1, has_side_effects=True, vmem_limit_bytes=VLIM
        ),
    )(slot_src, con, oa)


def increment_kernel(slots, blk_ref, got_ref, x_ref, innov_ref, band_ref, out_ref, proj):
    i = pl.program_id(0)
    lev, mem, chunk = x_ref.shape
    first = lax.axis_index("lev") * lev

    @pl.when(i == 0)
    def _():
        proj[...] = jnp.zeros_like(proj)

        def put(s, carry):
            blk = blk_ref[s]

            @pl.when(blk >= 0)
            def _():
                at = pl.ds(pl.multiple_of(blk * 128, 128), 128)
                for h in range(2):
                    proj[h * HALF : (h + 1) * HALF, at] += got_ref[h, s].astype(jnp.float32)

            return carry

        lax.fori_loop(0, slots, put, 0)

    at = pl.ds(pl.multiple_of(i * chunk, chunk), chunk)
    p = proj[:, at]
    var = jnp.sum(p * p, axis=0, keepdims=True) / (MEM - 1) + 0.1
    scale = innov_ref[...] / var / (MEM - 1)
    band = band_ref[...].astype(jnp.float32)
    p = p[:mem]
    for level in range(lev):
        cov = jnp.sum(x_ref[level].astype(jnp.float32) * p, axis=0, keepdims=True)
        dist = jnp.abs((first + level).astype(jnp.float32) - band)
        taper = jnp.maximum(0.0, 1.0 - dist / LTAP)
        out_ref[level : level + 1, :] = taper * cov * scale


def ocean_increment(blk, got, ocn_anom, innov, band, chunk):
    lev, mem, cells = ocn_anom.shape
    slots = got.shape[1]
    return pl.pallas_call(
        functools.partial(increment_kernel, slots),
        grid_spec=pltpu.PrefetchScalarGridSpec(
            num_scalar_prefetch=1,
            grid=(cells // chunk,),
            in_specs=[
                pl.BlockSpec(got.shape, lambda i, s: (0, 0, 0, 0)),
                pl.BlockSpec((lev, mem, chunk), lambda i, s: (0, 0, i)),
                pl.BlockSpec((1, chunk), lambda i, s: (0, i)),
                pl.BlockSpec((1, chunk), lambda i, s: (0, i)),
            ],
            out_specs=pl.BlockSpec((lev, chunk), lambda i, s: (0, i)),
            scratch_shapes=[pltpu.VMEM((2 * HALF, cells), jnp.float32)],
        ),
        out_shape=jax.ShapeDtypeStruct((lev, cells), jnp.float32),
        compiler_params=pltpu.CompilerParams(vmem_limit_bytes=VLIM),
        cost_estimate=pl.CostEstimate(
            flops=2 * lev * mem * cells, bytes_accessed=2 * lev * mem * cells, transcendentals=0
        ),
    )(blk, got, ocn_anom, innov.reshape(1, -1), band.reshape(1, -1))


def taper_levels(first, levels, band):
    lvl = (first + jnp.arange(levels, dtype=jnp.int32)).astype(jnp.float32)[:, None]
    return jnp.maximum(0.0, 1.0 - jnp.abs(lvl - band[None, :].astype(jnp.float32)) / LTAP)


def increment(anom, proj, tapered, innov):
    cov = jnp.sum(anom.astype(jnp.float32) * proj[None], axis=1) / (MEM - 1)
    var = jnp.sum(proj * proj, axis=0) / (MEM - 1) + 0.1
    return tapered * cov * (innov / var)[None, :]


def shards(
    atm_anom,
    ocn_anom,
    remap_w,
    rem_tile,
    rem_block,
    obs_weight,
    innov_ocn,
    innov_atm,
    band_ocn,
    band_atm,
):
    nt = lax.axis_size("tiles")
    lev = lax.axis_index("lev")
    alev, _, acells = atm_anom.shape
    nrem = remap_w.shape[0]
    per = max(2, 2 * ((nrem + nt - 1) // nt))
    slots = nt * per
    dest = rem_tile[:, 0]
    match_dest = (dest[:, None] == jnp.arange(nt, dtype=jnp.int32)[None, :]).astype(jnp.int32)
    rank = jnp.sum(jnp.cumsum(match_dest, axis=0) * match_dest, axis=1) - 1
    slot_of = dest * per + rank
    match_slot = (slot_of[None, :] == jnp.arange(slots, dtype=jnp.int32)[:, None]).astype(jnp.int32)
    slot_src = jnp.sum(match_slot * jnp.arange(nrem, dtype=jnp.int32)[None, :], axis=1)
    send_blk = jnp.sum(match_slot * (rem_block + 1)[None, :], axis=1) - 1
    idx = jnp.broadcast_to(send_blk.reshape(nt, per, 1), (nt, per, 128))
    idx = jnp.where(jnp.arange(128) == 0, jnp.maximum(idx, 0), idx)
    idx = jnp.pad(idx, ((0, 0), (0, 8 - per), (0, 0)))
    part = layer_parts(ocn_anom, 2048)
    lay, obs, blk = answers(part, idx, obs_weight, nt, per)
    con, oa = remap(slot_of, atm_anom, remap_w, lay, obs, 4)
    got, oa2 = give_back(slot_src, con, oa, nt, per)
    blk = blk[:, :per, 1].reshape(slots)
    got = got.reshape(2, slots, HALF, 128)
    ocn_increment = ocean_increment(blk, got, ocn_anom, innov_ocn, band_ocn, 2048)
    ocn_on_atm = oa2.reshape(2 * HALF, acells)[:MEM]
    taper_atm = taper_levels(lev * alev, alev, band_atm)
    atm_increment = increment(atm_anom, ocn_on_atm, taper_atm, innov_atm)
    return (ocn_increment, atm_increment)


def solution(mesh):
    in_specs = (
        P("lev", None, "tiles"),
        P("lev", None, "tiles"),
        P("tiles", None, None),
        P("tiles", None),
        P("tiles"),
        P("lev", "tiles"),
        P("tiles"),
        P("tiles"),
        P("tiles"),
        P("tiles"),
    )
    out_specs = (P("lev", "tiles"), P("lev", "tiles"))
    return jax.shard_map(shards, mesh=mesh, in_specs=in_specs, out_specs=out_specs, check_vma=False)
```

```python
import functools

import jax
import jax.numpy as jnp
from jax import lax
from jax.experimental import pallas as pl
from jax.experimental.pallas import tpu as pltpu
from jax.sharding import PartitionSpec as P

MEM = 30
HALF = 16
OLEV = 20
LTAP = 8
MESH = pl.DeviceIdType.MESH
VLIM = 56 * 1024 * 1024


def greet(nt, me, lev):
    barrier = pltpu.get_barrier_semaphore()

    def signal(k, carry):
        pl.semaphore_signal(
            barrier, inc=1, device_id=(lax.rem(me + k, nt), lev), device_id_type=MESH
        )
        return carry

    lax.fori_loop(1, nt, signal, 0)
    pl.semaphore_signal(barrier, inc=1, device_id=(me, 1 - lev), device_id_type=MESH)
    pl.semaphore_wait(barrier, nt)


def loop(first, last, fn):
    def body(k, carry):
        fn(k)
        return carry

    lax.fori_loop(first, last, body, 0)


def lanes(o, width=128):
    return pl.ds(pl.multiple_of(o * width, width), width)


def main_kernel(
    nt, per, chunk, parts,
    slot_ref, src_ref, idx_ref, obs_ref, ocn_hbm, atm_hbm, rw_hbm,
    got_ref, oa_ref, blk_ref,
    ocn, atm, rw, part, peer, layer, obs, lay_out, lay_rx, w_out, w_rx, obs_rx,
    xs, con, con_peer, summed, out, blk_smem,
    ocn_sem, atm_sem, rw_sem, smem_sem, swap_s, swap_r, con_s, con_r, oa_sem,
    idx_s, idx_r, w_s, w_r, lay_s, lay_r, out_s, out_r, fwd_s, fwd_r,
):
    me, lev = lax.axis_index("tiles"), lax.axis_index("lev")
    partner = (me, 1 - lev)
    alev = atm.shape[0]
    nrem = rw.shape[0]
    ablk = atm.shape[2] // 128
    rpb = nrem // ablk
    nchunk = ocn_hbm.shape[2] // chunk

    def fetch(i):
        return pltpu.make_async_copy(
            ocn_hbm.at[:, :, lanes(i, chunk)], ocn.at[lax.rem(i, 2)], ocn_sem.at[lax.rem(i, 2)]
        )

    fetch(0).start()
    atm_copy = pltpu.make_async_copy(atm_hbm, atm, atm_sem)
    rw_copy = pltpu.make_async_copy(rw_hbm, rw, rw_sem)
    greet(nt, me, lev)

    def move(src, dst, send, recv, k):
        to = lax.rem(me + k, nt)
        return pltpu.make_async_remote_copy(
            src_ref=src.at[to], dst_ref=dst.at[me], send_sem=send.at[k], recv_sem=recv.at[k],
            device_id=(to, lev), device_id_type=MESH,
        )

    def arrival(src, dst, send, recv, k):
        frm = lax.rem(me + nt - k, nt)
        return pltpu.make_async_remote_copy(
            src_ref=src.at[frm], dst_ref=dst.at[frm], send_sem=send.at[k], recv_sem=recv.at[k],
            device_id=(frm, lev), device_id_type=MESH,
        )

    idx_set = (idx_ref, blk_ref, idx_s, idx_r)
    w_set = (w_out, w_rx, w_s, w_r)
    lay_set = (lay_out, lay_rx, lay_s, lay_r)
    out_set = (out, got_ref.at[lev], out_s, out_r)

    loop(1, nt, lambda k: move(*idx_set, k).start())
    blk_ref[me] = idx_ref[me]

    def swap(i):
        at = lanes(i, chunk)
        return pltpu.make_async_remote_copy(
            src_ref=part.at[1 - lev, :, at], dst_ref=peer.at[:, at], send_sem=swap_s.at[i],
            recv_sem=swap_r.at[i], device_id=partner, device_id_type=MESH,
        )

    def layer_sum(i, more=True):
        if more:
            fetch(i + 1).start()
        fetch(i).wait()
        now = lax.rem(i, 2)
        sub = 256

        def piece(j):
            here = lanes(j, sub)
            at = pl.ds(pl.multiple_of(i * chunk + j * sub, sub), sub)
            total = ocn[now, 0, :, here].astype(jnp.float32)
            for level in range(1, ocn.shape[1]):
                total = total + ocn[now, level, :, here].astype(jnp.float32)
            part[0, :, at] = total[:HALF]
            part[1, : MEM - HALF, at] = total[HALF:]
            part[1, MEM - HALF :, at] = jnp.zeros((2 * HALF - MEM, sub), jnp.float32)

        loop(0, chunk // sub, piece)
        swap(i).start()

    early = nchunk // 3
    loop(0, early, layer_sum)

    def widen(o):
        obs[o] = obs_ref[:, lanes(o)].astype(jnp.float32)

    loop(0, obs.shape[0], widen)
    loop(1, nt, lambda k: arrival(*idx_set, k).wait_recv())
    loop(1, nt, lambda k: move(*idx_set, k).wait_send())
    down = pltpu.make_async_copy(blk_ref, blk_smem, smem_sem)
    down.start()
    down.wait()

    def fill_w(to, dst):
        for s in range(0, per, 2):
            pair = [obs[blk_smem[to, s + j, 0]] for j in range(2)]
            dst[to, 8 * s : 8 * s + 16, :] = jnp.concatenate(pair, axis=0).astype(jnp.bfloat16)

    def fill_lay(to, dst):
        for s in range(per):
            dst[to, HALF * s : HALF * (s + 1), :] = layer[blk_smem[to, s, 0]]

    def send_w(k):
        fill_w(lax.rem(me + k, nt), w_out)
        move(*w_set, k).start()

    loop(1, nt, send_w)
    fill_w(me, w_rx)
    loop(early, nchunk - 1, layer_sum)
    layer_sum(nchunk - 1, False)
    atm_copy.start()
    rw_copy.start()
    xs[...] = jnp.zeros_like(xs)

    def mean(i):
        swap(i).wait()

        def one(j):
            o = i * (chunk // 128) + j
            at = lanes(o)
            layer[o] = ((part[lev, :, at] + peer[:, at]) / OLEV).astype(jnp.bfloat16)

        loop(0, chunk // 128, one)

    loop(0, nchunk, mean)

    def send_lay(k):
        fill_lay(lax.rem(me + k, nt), lay_out)
        move(*lay_set, k).start()

    loop(1, nt, send_lay)
    for s in range(per):
        lay_rx[me, HALF * s : HALF * (s + 1), :] = layer[blk_smem[me, s, 0]]
    atm_copy.wait()
    rw_copy.wait()
    loop(1, nt, lambda k: arrival(*w_set, k).wait_recv())

    def spread(t):
        for s in range(0, per, 2):
            pair = w_rx[t, 8 * s : 8 * s + 16, :].astype(jnp.float32)
            obs_rx[t * per + s] = pair[:8]
            obs_rx[t * per + s + 1] = pair[8:]

    loop(0, nt, spread)

    def weights(b):
        return jnp.concatenate([rw[b * rpb + r] for r in range(rpb)], axis=1)

    def remap(b):
        xs[:, :MEM, :] = atm[:, :, lanes(b)]
        y = jnp.dot(
            xs[...].reshape(alev * 2 * HALF, 128), weights(b), preferred_element_type=jnp.float32
        )
        y = y.astype(jnp.bfloat16).astype(jnp.float32).reshape(alev, 2 * HALF, rpb * 128)
        local = jnp.concatenate([obs_rx[slot_ref[b * rpb + r]] for r in range(rpb)], axis=1)
        total = y[0] * local[0:1]
        for level in range(1, alev):
            total = total + y[level] * local[level : level + 1]
        for r in range(rpb):
            for h in range(2):
                con[h, b * rpb + r] = total[h * HALF : (h + 1) * HALF, 128 * r : 128 * (r + 1)]

    def con_swap(c):
        at = pl.ds(c * (nrem // parts), nrem // parts)
        return pltpu.make_async_remote_copy(
            src_ref=con.at[1 - lev, at], dst_ref=con_peer.at[at], send_sem=con_s.at[c],
            recv_sem=con_r.at[c], device_id=partner, device_id_type=MESH,
        )

    def remap_part(c):
        loop(c * (ablk // parts), (c + 1) * (ablk // parts), remap)
        con_swap(c).start()

    loop(0, parts, remap_part)

    def add(c):
        con_swap(c).wait()

        def four(j):
            at = pl.ds(c * (nrem // parts) + j * 4, 4)
            summed[at] = (con[lev, at] + con_peer[at]).astype(jnp.bfloat16)

        loop(0, nrem // parts // 4, four)

    loop(0, parts, add)

    def send_out(k):
        to = lax.rem(me + k, nt)
        for s in range(per):
            out[to, s * HALF : (s + 1) * HALF, :] = summed[src_ref[to * per + s]]
        move(*out_set, k).start()

    loop(1, nt, send_out)
    for s in range(per):
        got_ref[lev, me, s * HALF : (s + 1) * HALF, :] = summed[src_ref[me * per + s]]

    def forward(k, half):
        frm = lax.rem(me + nt - k, nt)
        return pltpu.make_async_remote_copy(
            src_ref=got_ref.at[half, frm], dst_ref=got_ref.at[half, frm], send_sem=fwd_s.at[k],
            recv_sem=fwd_r.at[k], device_id=partner, device_id_type=MESH,
        )

    forward(0, lev).start()
    loop(1, nt, lambda k: arrival(*lay_set, k).wait_recv())

    def split(t):
        for s in range(per):
            layer[t * per + s] = lay_rx[t, HALF * s : HALF * (s + 1), :]

    loop(1, nt, lambda k: move(*lay_set, k).wait_send())
    loop(0, nt, split)

    def back(b):
        lay = jnp.concatenate([layer[slot_ref[b * rpb + r]] for r in range(rpb)], axis=1)
        oa_ref[lev, :, lanes(b)] = lax.dot_general(
            lay, weights(b), (((1,), (1,)), ((), ())), preferred_element_type=jnp.float32
        )

    loop(0, ablk, back)
    oa_swap = pltpu.make_async_remote_copy(
        src_ref=oa_ref.at[lev], dst_ref=oa_ref.at[lev], send_sem=oa_sem.at[0],
        recv_sem=oa_sem.at[1], device_id=partner, device_id_type=MESH,
    )
    oa_swap.start()

    def pass_on(k):
        arrival(*out_set, k).wait_recv()
        forward(k, lev).start()

    loop(1, nt, pass_on)

    def finish(k):
        forward(k, 1 - lev).wait_recv()
        forward(k, lev).wait_send()

    loop(0, nt, finish)
    loop(1, nt, lambda k: move(*out_set, k).wait_send())
    loop(1, nt, lambda k: move(*w_set, k).wait_send())
    oa_swap.wait_send()
    pltpu.make_async_remote_copy(
        src_ref=oa_ref.at[1 - lev], dst_ref=oa_ref.at[1 - lev], send_sem=oa_sem.at[0],
        recv_sem=oa_sem.at[1], device_id=partner, device_id_type=MESH,
    ).wait_recv()


def exchange(slot_of, slot_src, idx, obs, ocn_anom, atm_anom, remap_w, nt, per):
    chunk, parts = 2048, 4
    olev, mem, cells = ocn_anom.shape
    alev, _, acells = atm_anom.shape
    nrem = remap_w.shape[0]
    oblk = cells // 128
    slots = nt * per
    vmem = pl.BlockSpec(memory_space=pltpu.VMEM)
    smem = pl.BlockSpec(memory_space=pltpu.SMEM)
    hbm = pl.BlockSpec(memory_space=pl.ANY)
    dma = pltpu.SemaphoreType.DMA
    f32, bf16, i32 = jnp.float32, jnp.bfloat16, jnp.int32
    return pl.pallas_call(
        functools.partial(main_kernel, nt, per, chunk, parts),
        out_shape=(
            jax.ShapeDtypeStruct((2, nt, per * HALF, 128), bf16),
            jax.ShapeDtypeStruct((2, HALF, acells), f32),
            jax.ShapeDtypeStruct((nt, 8, 128), i32),
        ),
        in_specs=[smem, smem, vmem, vmem, hbm, hbm, hbm],
        out_specs=(vmem,) * 3,
        scratch_shapes=[
            pltpu.VMEM((2, olev, mem, chunk), bf16),
            pltpu.VMEM(atm_anom.shape, bf16),
            pltpu.VMEM(remap_w.shape, bf16),
            pltpu.VMEM((2, HALF, cells), f32),
            pltpu.VMEM((HALF, cells), f32),
            pltpu.VMEM((max(oblk, slots), HALF, 128), bf16),
            pltpu.VMEM((oblk, 8, 128), f32),
            pltpu.VMEM((nt, per * HALF, 128), bf16),
            pltpu.VMEM((nt, per * HALF, 128), bf16),
            pltpu.VMEM((nt, per * 8, 128), bf16),
            pltpu.VMEM((nt, per * 8, 128), bf16),
            pltpu.VMEM((slots, 8, 128), f32),
            pltpu.VMEM((alev, 2 * HALF, 128), bf16),
            pltpu.VMEM((2, nrem, HALF, 128), f32),
            pltpu.VMEM((nrem, HALF, 128), f32),
            pltpu.VMEM((nrem, HALF, 128), bf16),
            pltpu.VMEM((nt, per * HALF, 128), bf16),
            pltpu.SMEM((nt, 8, 128), i32),
            dma((2,)), dma, dma, dma,
            dma((cells // chunk,)), dma((cells // chunk,)),
            dma((parts,)), dma((parts,)), dma((2,)),
        ]
        + [dma((nt,))] * 10,
        compiler_params=pltpu.CompilerParams(
            collective_id=0, has_side_effects=True, vmem_limit_bytes=VLIM
        ),
    )(slot_of, slot_src, idx, obs, ocn_anom, atm_anom, remap_w)


def increment_kernel(per, blk_ref, got_ref, x_ref, innov_ref, band_ref, out_ref, proj):
    i = pl.program_id(0)
    lev, mem, chunk = x_ref.shape
    first = lax.axis_index("lev") * lev

    @pl.when(i == 0)
    def _():
        proj[...] = jnp.zeros_like(proj)

        def put(s, carry):
            blk = blk_ref[s // per, s % per, 1]

            @pl.when(blk >= 0)
            def _():
                at = pl.ds(pl.multiple_of(blk * 128, 128), 128)
                for h in range(2):
                    proj[h * HALF : (h + 1) * HALF, at] += got_ref[h, s].astype(jnp.float32)

            return carry

        lax.fori_loop(0, got_ref.shape[1], put, 0)

    sub = 256

    def piece(j, carry):
        here = pl.ds(pl.multiple_of(j * sub, sub), sub)
        p = proj[:, pl.ds(pl.multiple_of(i * chunk + j * sub, sub), sub)]
        var = jnp.sum(p * p, axis=0, keepdims=True) / (MEM - 1) + 0.1
        scale = innov_ref[:, here] / var / (MEM - 1)
        band = band_ref[:, here].astype(jnp.float32)
        p = p[:mem]
        for level in range(lev):
            cov = jnp.sum(x_ref[level, :, here].astype(jnp.float32) * p, axis=0, keepdims=True)
            dist = jnp.abs((first + level).astype(jnp.float32) - band)
            taper = jnp.maximum(0.0, 1.0 - dist / LTAP)
            out_ref[level : level + 1, here] = taper * cov * scale
        return carry

    lax.fori_loop(0, chunk // sub, piece, 0)


def ocean_increment(blk, got, ocn_anom, innov, band, chunk):
    lev, mem, cells = ocn_anom.shape
    slots = got.shape[1]
    return pl.pallas_call(
        functools.partial(increment_kernel, slots // blk.shape[0]),
        grid=(cells // chunk,),
        in_specs=[
            pl.BlockSpec(memory_space=pltpu.SMEM),
            pl.BlockSpec(got.shape, lambda i: (0, 0, 0, 0)),
            pl.BlockSpec((lev, mem, chunk), lambda i: (0, 0, i)),
            pl.BlockSpec((1, chunk), lambda i: (0, i)),
            pl.BlockSpec((1, chunk), lambda i: (0, i)),
        ],
        out_specs=pl.BlockSpec((lev, chunk), lambda i: (0, i)),
        scratch_shapes=[pltpu.VMEM((2 * HALF, cells), jnp.float32)],
        out_shape=jax.ShapeDtypeStruct((lev, cells), jnp.float32),
        compiler_params=pltpu.CompilerParams(vmem_limit_bytes=VLIM),
        cost_estimate=pl.CostEstimate(
            flops=2 * lev * mem * cells, bytes_accessed=2 * lev * mem * cells, transcendentals=0
        ),
    )(blk, got, ocn_anom, innov.reshape(1, -1), band.reshape(1, -1))


def taper_levels(first, levels, band):
    lvl = (first + jnp.arange(levels, dtype=jnp.int32)).astype(jnp.float32)[:, None]
    return jnp.maximum(0.0, 1.0 - jnp.abs(lvl - band[None, :].astype(jnp.float32)) / LTAP)


def increment(anom, proj, tapered, innov):
    cov = jnp.sum(anom.astype(jnp.float32) * proj[None], axis=1) / (MEM - 1)
    var = jnp.sum(proj * proj, axis=0) / (MEM - 1) + 0.1
    return tapered * cov * (innov / var)[None, :]


def shards(
    atm_anom,
    ocn_anom,
    remap_w,
    rem_tile,
    rem_block,
    obs_weight,
    innov_ocn,
    innov_atm,
    band_ocn,
    band_atm,
):
    nt = lax.axis_size("tiles")
    lev = lax.axis_index("lev")
    alev, _, acells = atm_anom.shape
    nrem = remap_w.shape[0]
    per = max(2, 2 * ((nrem + nt - 1) // nt))
    slots = nt * per
    dest = rem_tile[:, 0]
    match_dest = (dest[:, None] == jnp.arange(nt, dtype=jnp.int32)[None, :]).astype(jnp.int32)
    rank = jnp.sum(jnp.cumsum(match_dest, axis=0) * match_dest, axis=1) - 1
    slot_of = dest * per + rank
    match_slot = (slot_of[None, :] == jnp.arange(slots, dtype=jnp.int32)[:, None]).astype(jnp.int32)
    slot_src = jnp.sum(match_slot * jnp.arange(nrem, dtype=jnp.int32)[None, :], axis=1)
    send_blk = jnp.sum(match_slot * (rem_block + 1)[None, :], axis=1) - 1
    idx = jnp.broadcast_to(send_blk.reshape(nt, per, 1), (nt, per, 128))
    idx = jnp.where(jnp.arange(128) == 0, jnp.maximum(idx, 0), idx)
    idx = jnp.pad(idx, ((0, 0), (0, 8 - per), (0, 0)))
    got, oa2, blk = exchange(
        slot_of, slot_src, idx, obs_weight, ocn_anom, atm_anom, remap_w, nt, per
    )
    got = got.reshape(2, slots, HALF, 128)
    ocn_increment = ocean_increment(blk, got, ocn_anom, innov_ocn, band_ocn, 2048)
    ocn_on_atm = oa2.reshape(2 * HALF, acells)[:MEM]
    taper_atm = taper_levels(lev * alev, alev, band_atm)
    atm_increment = increment(atm_anom, ocn_on_atm, taper_atm, innov_atm)
    return (ocn_increment, atm_increment)


def solution(mesh):
    in_specs = (
        P("lev", None, "tiles"),
        P("lev", None, "tiles"),
        P("tiles", None, None),
        P("tiles", None),
        P("tiles"),
        P("lev", "tiles"),
        P("tiles"),
        P("tiles"),
        P("tiles"),
        P("tiles"),
    )
    out_specs = (P("lev", "tiles"), P("lev", "tiles"))
    return jax.shard_map(shards, mesh=mesh, in_specs=in_specs, out_specs=out_specs, check_vma=False)
```

```python
import functools

import jax
import jax.numpy as jnp
from jax import lax
from jax.experimental import pallas as pl
from jax.experimental.pallas import tpu as pltpu
from jax.sharding import PartitionSpec as P

MEM = 30
HALF = 16
OLEV = 20
LTAP = 8
MESH = pl.DeviceIdType.MESH
VLIM = 56 * 1024 * 1024


def greet(nt, me, lev):
    barrier = pltpu.get_barrier_semaphore()

    def signal(k, carry):
        pl.semaphore_signal(
            barrier, inc=1, device_id=(lax.rem(me + k, nt), lev), device_id_type=MESH
        )
        return carry

    lax.fori_loop(1, nt, signal, 0)
    pl.semaphore_signal(barrier, inc=1, device_id=(me, 1 - lev), device_id_type=MESH)
    pl.semaphore_wait(barrier, nt)


def loop(first, last, fn):
    def body(k, carry):
        fn(k)
        return carry

    lax.fori_loop(first, last, body, 0)


def lanes(o, width=128):
    return pl.ds(pl.multiple_of(o * width, width), width)


def main_kernel(
    nt, per, chunk, parts,
    slot_ref, src_ref, idx_ref, obs_ref, innov_ref, band_ref, ocn_hbm, atm_hbm, rw_hbm,
    got_ref, inc_ref, blk_ref,
    oa_ref,
    ocn, atm, rw, part, peer, layer, obs, lay_out, lay_rx, w_out, w_rx, obs_rx,
    con, con_peer, summed, out, blk_smem,
    ocn_sem, atm_sem, rw_sem, smem_sem, swap_s, swap_r, con_s, con_r, oa_sem,
    idx_s, idx_r, w_s, w_r, lay_s, lay_r, out_s, out_r, fwd_s, fwd_r,
):
    me, lev = lax.axis_index("tiles"), lax.axis_index("lev")
    partner = (me, 1 - lev)
    alev = obs_ref.shape[0]
    nrem = rw.shape[0]
    ablk = atm.shape[1] // 128
    rpb = nrem // ablk
    nchunk = ocn_hbm.shape[2] // chunk

    def fetch(i):
        return pltpu.make_async_copy(
            ocn_hbm.at[:, :, lanes(i, chunk)], ocn.at[lax.rem(i, 2)], ocn_sem.at[lax.rem(i, 2)]
        )

    fetch(0).start()
    atm_copy = pltpu.make_async_copy(atm_hbm, atm, atm_sem)
    rw_copy = pltpu.make_async_copy(rw_hbm, rw, rw_sem)
    greet(nt, me, lev)

    def move(src, dst, send, recv, k):
        to = lax.rem(me + k, nt)
        return pltpu.make_async_remote_copy(
            src_ref=src.at[to], dst_ref=dst.at[me], send_sem=send.at[k], recv_sem=recv.at[k],
            device_id=(to, lev), device_id_type=MESH,
        )

    def arrival(src, dst, send, recv, k):
        frm = lax.rem(me + nt - k, nt)
        return pltpu.make_async_remote_copy(
            src_ref=src.at[frm], dst_ref=dst.at[frm], send_sem=send.at[k], recv_sem=recv.at[k],
            device_id=(frm, lev), device_id_type=MESH,
        )

    idx_set = (idx_ref, blk_ref, idx_s, idx_r)
    w_set = (w_out, w_rx, w_s, w_r)
    lay_set = (lay_out, lay_rx, lay_s, lay_r)
    out_set = (out, got_ref.at[lev], out_s, out_r)

    loop(1, nt, lambda k: move(*idx_set, k).start())
    blk_ref[me] = idx_ref[me]

    def swap(i):
        at = lanes(i, chunk)
        return pltpu.make_async_remote_copy(
            src_ref=part.at[1 - lev, :, at], dst_ref=peer.at[:, at], send_sem=swap_s.at[i],
            recv_sem=swap_r.at[i], device_id=partner, device_id_type=MESH,
        )

    def layer_sum(i, more=True):
        if more:
            fetch(i + 1).start()
        fetch(i).wait()
        now = lax.rem(i, 2)
        sub = 256

        def piece(j):
            here = lanes(j, sub)
            at = pl.ds(pl.multiple_of(i * chunk + j * sub, sub), sub)
            total = ocn[now, 0, :, here].astype(jnp.float32)
            for level in range(1, ocn.shape[1]):
                total = total + ocn[now, level, :, here].astype(jnp.float32)
            part[0, :, at] = total[:HALF]
            part[1, : MEM - HALF, at] = total[HALF:]
            part[1, MEM - HALF :, at] = jnp.zeros((2 * HALF - MEM, sub), jnp.float32)

        loop(0, chunk // sub, piece)
        swap(i).start()

    early = nchunk // 3
    loop(0, early, layer_sum)

    def widen(o):
        obs[o] = obs_ref[:, lanes(o)].astype(jnp.float32)

    loop(0, obs.shape[0], widen)
    loop(1, nt, lambda k: arrival(*idx_set, k).wait_recv())
    loop(1, nt, lambda k: move(*idx_set, k).wait_send())
    down = pltpu.make_async_copy(blk_ref, blk_smem, smem_sem)
    down.start()
    down.wait()

    def fill_w(to, dst):
        for s in range(0, per, 2):
            pair = [obs[blk_smem[to, s + j, 0]] for j in range(2)]
            dst[to, 8 * s : 8 * s + 16, :] = jnp.concatenate(pair, axis=0).astype(jnp.bfloat16)

    def fill_lay(to, dst):
        for s in range(per):
            dst[to, HALF * s : HALF * (s + 1), :] = layer[blk_smem[to, s, 0]]

    def send_w(k):
        fill_w(lax.rem(me + k, nt), w_out)
        move(*w_set, k).start()

    loop(1, nt, send_w)
    fill_w(me, w_rx)
    loop(early, nchunk - 1, layer_sum)
    layer_sum(nchunk - 1, False)
    atm_copy.start()
    rw_copy.start()

    def mean(i):
        swap(i).wait()

        def one(j):
            o = i * (chunk // 128) + j
            at = lanes(o)
            layer[o] = ((part[lev, :, at] + peer[:, at]) / OLEV).astype(jnp.bfloat16)

        loop(0, chunk // 128, one)

    loop(0, nchunk, mean)

    def send_lay(k):
        fill_lay(lax.rem(me + k, nt), lay_out)
        move(*lay_set, k).start()

    loop(1, nt, send_lay)
    for s in range(per):
        lay_rx[me, HALF * s : HALF * (s + 1), :] = layer[blk_smem[me, s, 0]]
    atm_copy.wait()
    rw_copy.wait()
    loop(1, nt, lambda k: arrival(*w_set, k).wait_recv())

    def spread(t):
        for s in range(0, per, 2):
            pair = w_rx[t, 8 * s : 8 * s + 16, :].astype(jnp.float32)
            obs_rx[t * per + s] = pair[:8]
            obs_rx[t * per + s + 1] = pair[8:]

    loop(0, nt, spread)

    def weights(b):
        return jnp.concatenate([rw[b * rpb + r] for r in range(rpb)], axis=1)

    def remap(b):
        y = jnp.dot(atm[:, lanes(b)], weights(b), preferred_element_type=jnp.float32)
        y = y.astype(jnp.bfloat16).astype(jnp.float32).reshape(MEM, alev, rpb * 128)
        local = jnp.concatenate([obs_rx[slot_ref[b * rpb + r]] for r in range(rpb)], axis=1)
        total = jnp.sum(y * local[None], axis=1)
        total = jnp.concatenate(
            [total, jnp.zeros((2 * HALF - MEM, rpb * 128), jnp.float32)], axis=0
        )
        for r in range(rpb):
            for h in range(2):
                con[h, b * rpb + r] = total[h * HALF : (h + 1) * HALF, 128 * r : 128 * (r + 1)]

    def con_swap(c):
        at = pl.ds(c * (nrem // parts), nrem // parts)
        return pltpu.make_async_remote_copy(
            src_ref=con.at[1 - lev, at], dst_ref=con_peer.at[at], send_sem=con_s.at[c],
            recv_sem=con_r.at[c], device_id=partner, device_id_type=MESH,
        )

    def remap_part(c):
        loop(c * (ablk // parts), (c + 1) * (ablk // parts), remap)
        con_swap(c).start()

    loop(0, parts, remap_part)

    def add(c):
        con_swap(c).wait()

        def four(j):
            at = pl.ds(c * (nrem // parts) + j * 4, 4)
            summed[at] = (con[lev, at] + con_peer[at]).astype(jnp.bfloat16)

        loop(0, nrem // parts // 4, four)

    loop(0, parts, add)

    def send_out(k):
        to = lax.rem(me + k, nt)
        for s in range(per):
            out[to, s * HALF : (s + 1) * HALF, :] = summed[src_ref[to * per + s]]
        move(*out_set, k).start()

    loop(1, nt, send_out)
    for s in range(per):
        got_ref[lev, me, s * HALF : (s + 1) * HALF, :] = summed[src_ref[me * per + s]]

    def forward(k, half):
        frm = lax.rem(me + nt - k, nt)
        return pltpu.make_async_remote_copy(
            src_ref=got_ref.at[half, frm], dst_ref=got_ref.at[half, frm], send_sem=fwd_s.at[k],
            recv_sem=fwd_r.at[k], device_id=partner, device_id_type=MESH,
        )

    forward(0, lev).start()
    loop(1, nt, lambda k: arrival(*lay_set, k).wait_recv())

    def split(t):
        for s in range(per):
            layer[t * per + s] = lay_rx[t, HALF * s : HALF * (s + 1), :]

    loop(1, nt, lambda k: move(*lay_set, k).wait_send())
    loop(0, nt, split)

    def back(b):
        lay = jnp.concatenate([layer[slot_ref[b * rpb + r]] for r in range(rpb)], axis=1)
        oa_ref[lev, :, lanes(b)] = lax.dot_general(
            lay, weights(b), (((1,), (1,)), ((), ())), preferred_element_type=jnp.float32
        )

    loop(0, ablk, back)
    oa_swap = pltpu.make_async_remote_copy(
        src_ref=oa_ref.at[lev], dst_ref=oa_ref.at[lev], send_sem=oa_sem.at[0],
        recv_sem=oa_sem.at[1], device_id=partner, device_id_type=MESH,
    )
    oa_swap.start()
    oa_swap.wait_send()
    pltpu.make_async_remote_copy(
        src_ref=oa_ref.at[1 - lev], dst_ref=oa_ref.at[1 - lev], send_sem=oa_sem.at[0],
        recv_sem=oa_sem.at[1], device_id=partner, device_id_type=MESH,
    ).wait_recv()
    level = lev * alev + lax.broadcasted_iota(jnp.int32, (alev, 128), 0)

    def increment(b):
        at = lanes(b)
        halves = [oa_ref[0, :, at], oa_ref[1, :, at]]
        square = halves[0] * halves[0] + halves[1] * halves[1]
        var = jnp.sum(square, axis=0, keepdims=True) / (MEM - 1) + 0.1
        x = atm[:, at].astype(jnp.float32)
        cov = jnp.zeros((alev, 128), jnp.float32)
        for m in range(MEM):
            row = halves[m // HALF][m % HALF : m % HALF + 1]
            cov = cov + x[m * alev : (m + 1) * alev] * row
        dist = jnp.abs(level - band_ref[:, at]).astype(jnp.float32)
        taper = jnp.maximum(0.0, 1.0 - dist / LTAP)
        inc_ref[:, at] = taper * (cov / (MEM - 1)) * (innov_ref[:, at] / var)

    loop(0, ablk, increment)

    def pass_on(k):
        arrival(*out_set, k).wait_recv()
        forward(k, lev).start()

    loop(1, nt, pass_on)

    def finish(k):
        forward(k, 1 - lev).wait_recv()
        forward(k, lev).wait_send()

    loop(0, nt, finish)
    loop(1, nt, lambda k: move(*out_set, k).wait_send())
    loop(1, nt, lambda k: move(*w_set, k).wait_send())


def exchange(slot_of, slot_src, idx, obs, innov, band, ocn_anom, atm_anom, remap_w, nt, per):
    chunk, parts = 2048, 4
    olev, mem, cells = ocn_anom.shape
    alev, acells = obs.shape[0], atm_anom.shape[1]
    nrem = remap_w.shape[0]
    oblk = cells // 128
    slots = nt * per
    vmem = pl.BlockSpec(memory_space=pltpu.VMEM)
    smem = pl.BlockSpec(memory_space=pltpu.SMEM)
    hbm = pl.BlockSpec(memory_space=pl.ANY)
    dma = pltpu.SemaphoreType.DMA
    f32, bf16, i32 = jnp.float32, jnp.bfloat16, jnp.int32
    return pl.pallas_call(
        functools.partial(main_kernel, nt, per, chunk, parts),
        out_shape=(
            jax.ShapeDtypeStruct((2, nt, per * HALF, 128), bf16),
            jax.ShapeDtypeStruct((alev, acells), f32),
            jax.ShapeDtypeStruct((nt, 8, 128), i32),
        ),
        in_specs=[smem, smem, vmem, vmem, vmem, vmem, hbm, hbm, hbm],
        out_specs=(vmem,) * 3,
        scratch_shapes=[
            pltpu.VMEM((2, HALF, acells), f32),
            pltpu.VMEM((2, olev, mem, chunk), bf16),
            pltpu.VMEM(atm_anom.shape, bf16),
            pltpu.VMEM(remap_w.shape, bf16),
            pltpu.VMEM((2, HALF, cells), f32),
            pltpu.VMEM((HALF, cells), f32),
            pltpu.VMEM((max(oblk, slots), HALF, 128), bf16),
            pltpu.VMEM((oblk, 8, 128), f32),
            pltpu.VMEM((nt, per * HALF, 128), bf16),
            pltpu.VMEM((nt, per * HALF, 128), bf16),
            pltpu.VMEM((nt, per * 8, 128), bf16),
            pltpu.VMEM((nt, per * 8, 128), bf16),
            pltpu.VMEM((slots, 8, 128), f32),
            pltpu.VMEM((2, nrem, HALF, 128), f32),
            pltpu.VMEM((nrem, HALF, 128), f32),
            pltpu.VMEM((nrem, HALF, 128), bf16),
            pltpu.VMEM((nt, per * HALF, 128), bf16),
            pltpu.SMEM((nt, 8, 128), i32),
            dma((2,)), dma, dma, dma,
            dma((cells // chunk,)), dma((cells // chunk,)),
            dma((parts,)), dma((parts,)), dma((2,)),
        ]
        + [dma((nt,))] * 10,
        compiler_params=pltpu.CompilerParams(
            collective_id=0, has_side_effects=True, vmem_limit_bytes=VLIM
        ),
    )(slot_of, slot_src, idx, obs, innov, band, ocn_anom, atm_anom, remap_w)


def increment_kernel(
    per, blk_ref, got_ref, x_hbm, innov_ref, band_ref, out_ref, proj, x, place, held, sems
):
    lev, mem, cells = x_hbm.shape
    slots = got_ref.shape[1]
    level = lax.axis_index("lev") * lev + lax.broadcasted_iota(jnp.int32, (lev, 128), 0)

    def clear(o, carry):
        place[o] = -1
        return carry

    lax.fori_loop(0, cells // 128, clear, 0)

    def fetch(n):
        at = pl.ds(pl.multiple_of(held[n] * 128, 128), 128)
        return pltpu.make_async_copy(x_hbm.at[:, :, at], x.at[n], sems.at[n])

    def put(s, count):
        blk = blk_ref[s // per, s % per, 1]
        seen = place[jnp.maximum(blk, 0)]
        new = jnp.logical_and(blk >= 0, seen < 0)

        @pl.when(new)
        def _():
            place[blk] = count
            held[count] = blk
            fetch(count).start()
            for h in range(2):
                proj[count, h * HALF : (h + 1) * HALF] = got_ref[h, s].astype(jnp.float32)

        @pl.when(jnp.logical_and(blk >= 0, seen >= 0))
        def _():
            for h in range(2):
                proj[seen, h * HALF : (h + 1) * HALF] += got_ref[h, s].astype(jnp.float32)

        return count + new.astype(jnp.int32)

    count = lax.fori_loop(0, slots, put, 0)
    out_ref[...] = jnp.zeros_like(out_ref)

    def block(n, carry):
        at = pl.ds(pl.multiple_of(held[n] * 128, 128), 128)
        p = proj[n]
        var = jnp.sum(p * p, axis=0, keepdims=True) / (MEM - 1) + 0.1
        p = p[:mem]
        fetch(n).wait()
        cov = [
            jnp.sum(x[n, l].astype(jnp.float32) * p, axis=0, keepdims=True) for l in range(lev)
        ]
        cov = jnp.concatenate(cov, axis=0) / (MEM - 1)
        dist = jnp.abs(level - band_ref[:, at]).astype(jnp.float32)
        taper = jnp.maximum(0.0, 1.0 - dist / LTAP)
        out_ref[:, at] = taper * cov * (innov_ref[:, at] / var)
        return carry

    lax.fori_loop(0, count, block, 0)


def ocean_increment(blk, got, ocn_anom, innov, band):
    lev, mem, cells = ocn_anom.shape
    slots = got.shape[1]
    vmem = pl.BlockSpec(memory_space=pltpu.VMEM)
    return pl.pallas_call(
        functools.partial(increment_kernel, slots // blk.shape[0]),
        in_specs=[
            pl.BlockSpec(memory_space=pltpu.SMEM), vmem, pl.BlockSpec(memory_space=pl.ANY),
            vmem, vmem,
        ],
        out_specs=vmem,
        out_shape=jax.ShapeDtypeStruct((lev, cells), jnp.float32),
        scratch_shapes=[
            pltpu.VMEM((slots, 2 * HALF, 128), jnp.float32),
            pltpu.VMEM((slots, lev, mem, 128), jnp.bfloat16),
            pltpu.SMEM((cells // 128,), jnp.int32),
            pltpu.SMEM((slots,), jnp.int32),
            pltpu.SemaphoreType.DMA((slots,)),
        ],
        compiler_params=pltpu.CompilerParams(vmem_limit_bytes=VLIM),
        cost_estimate=pl.CostEstimate(
            flops=2 * lev * mem * cells, bytes_accessed=2 * lev * mem * cells, transcendentals=0
        ),
    )(blk, got, ocn_anom, innov.reshape(1, -1), band.reshape(1, -1))


def shards(
    atm_anom,
    ocn_anom,
    remap_w,
    rem_tile,
    rem_block,
    obs_weight,
    innov_ocn,
    innov_atm,
    band_ocn,
    band_atm,
):
    nt = lax.axis_size("tiles")
    acells = atm_anom.shape[2]
    nrem = remap_w.shape[0]
    per = max(2, 2 * ((nrem + nt - 1) // nt))
    slots = nt * per
    dest = rem_tile[:, 0]
    match_dest = (dest[:, None] == jnp.arange(nt, dtype=jnp.int32)[None, :]).astype(jnp.int32)
    rank = jnp.sum(jnp.cumsum(match_dest, axis=0) * match_dest, axis=1) - 1
    slot_of = dest * per + rank
    match_slot = (slot_of[None, :] == jnp.arange(slots, dtype=jnp.int32)[:, None]).astype(jnp.int32)
    slot_src = jnp.sum(match_slot * jnp.arange(nrem, dtype=jnp.int32)[None, :], axis=1)
    send_blk = jnp.sum(match_slot * (rem_block + 1)[None, :], axis=1) - 1
    idx = jnp.broadcast_to(send_blk.reshape(nt, per, 1), (nt, per, 128))
    idx = jnp.where(jnp.arange(128) == 0, jnp.maximum(idx, 0), idx)
    idx = jnp.pad(idx, ((0, 0), (0, 8 - per), (0, 0)))
    rows = atm_anom.transpose(1, 0, 2).reshape(-1, acells)
    got, atm_increment, blk = exchange(
        slot_of, slot_src, idx, obs_weight, innov_atm.reshape(1, -1), band_atm.reshape(1, -1),
        ocn_anom, rows, remap_w, nt, per,
    )
    got = got.reshape(2, slots, HALF, 128)
    ocn_increment = ocean_increment(blk, got, ocn_anom, innov_ocn, band_ocn)
    return (ocn_increment, atm_increment)


def solution(mesh):
    in_specs = (
        P("lev", None, "tiles"),
        P("lev", None, "tiles"),
        P("tiles", None, None),
        P("tiles", None),
        P("tiles"),
        P("lev", "tiles"),
        P("tiles"),
        P("tiles"),
        P("tiles"),
        P("tiles"),
    )
    out_specs = (P("lev", "tiles"), P("lev", "tiles"))
    return jax.shard_map(shards, mesh=mesh, in_specs=in_specs, out_specs=out_specs, check_vma=False)
```
